32 devices in a mesh: parts: 2 (over y), space: 16 (over z, x, core).
Axes of the slice: x: 2, y: 2, z: 4, core: 2. Of those that a mesh axis runs over, the one named last changes fastest.
Arguments:
- grid_latent: bfloat16 [8, 4096, 512], P(None, ('parts', 'space')), parts along dimension 1, may hold values from -6 to 6
- mesh_latent: bfloat16 [8, 1024, 512], P(None, ('parts', 'space')), parts along dimension 1, may hold values from -6 to 6
- send_rows: int32 [32, 16, 2], P(('parts', 'space')), parts along dimension 0, may hold values from 0 to 31
- edge_slot: int32 [3, 4096], P(None, ('parts', 'space')), parts along dimension 1, may hold values from 0 to 63, as said below
- lat_row: int32 [4096], P(('parts', 'space')), parts along dimension 0, may hold values from 0 to 720
- verifying_analyses: float32 [83, 4096], P(None, ('parts', 'space')), parts along dimension 1, may hold values from -6 to 6
- w_send: bfloat16 [512, 512], replicated, may hold values from -0.1875 to 0.1875
- w_recv: bfloat16 [512, 512], replicated, may hold values from -0.1875 to 0.1875
- w_edge: bfloat16 [512, 512], replicated, may hold values from -0.25 to 0.25
- edge_gain: float32 [512], replicated, may hold values from 0.1 to 1.9
- head_matrix: bfloat16 [512, 83], replicated, may hold values from -0.25 to 0.25
Outputs:
- loss: float32 [2], P('parts'), parts along dimension 0
- grad_grid: bfloat16 [8, 4096, 512], P(None, ('parts', 'space')), parts along dimension 1
- grad_mesh: bfloat16 [8, 1024, 512], P(None, ('parts', 'space')), parts along dimension 1
- grad_send: float32 [1024, 512], P('parts'), parts along dimension 0
- grad_recv: float32 [1024, 512], P('parts'), parts along dimension 0
- grad_edge: float32 [1024, 512], P('parts'), parts along dimension 0
- grad_gain: float32 [1024], P('parts'), parts along dimension 0
- head_matrix_sensitivity: float32 [1024, 83], P('parts'), parts along dimension 0
The draws below stay inside these ranges and needn't reach their ends.
There are 2 independent parts, one for each index of `parts`. The reference program is written for one: setup_inputs(seed, part) draws one part's arguments, and reference() takes and returns one part's arrays. A program takes and returns all parts, laid end to end along the dimension named above; an argument that names none is the same for every part. Nothing has to cross between parts.
Inputs may be any that keep to these rules, and one draw needn't show every extreme that they name: `edge_slot`: for a grid point of device q, a value v below 32 names row v of q's own block of mesh nodes; a value 32 + p * 2 + k names the mesh node in row send_rows[p, q, k] of device p's block. The neighbours of one point need not differ.
All inputs are finite; a program needn't handle non-finite values.
Results may differ from the reference program's by a relative error of at most 0.009.
The reference program's roundings to bfloat16 on the way count: a program that leaves them out, or rounds other values in their place, can miss the bound.
Values may be sent and summed in bfloat16 or wider, within the bound.
A program may use at most 128 MiB of HBM per device.

```python
import jax
import jax.numpy as jnp
from jax import lax

MEMBERS = 8
LATENT = 512
HIDDEN_SIZE = 512
CHANNELS = 83
NEI = 3
LATS = 721
CAP = 2
GP = 128
MN = 32
GRID = 2048
MESH = 512
N_SPACE = 16


def draw_edge_slot(key, part):
    key = jax.random.fold_in(key, 7)
    key_list = jax.random.split(key, 5)
    edge_count = NEI * GP
    slot_count = N_SPACE * CAP
    device = jnp.arange(N_SPACE, dtype=jnp.int32)
    counts = jax.random.randint(key_list[0], (N_SPACE, N_SPACE), 0, CAP + 1)
    counts = jnp.where(device[None, :] == (device[:, None] + 1) % N_SPACE, CAP, counts)
    counts = jnp.where(device[None, :] == device[:, None], 0, counts)
    position = jnp.arange(slot_count, dtype=jnp.int32)
    is_live = ((position % CAP)[None, :] < jnp.repeat(counts, CAP, axis=1)).astype(jnp.int32)
    live_order = jnp.argsort(1 - is_live, axis=1, stable=True).astype(jnp.int32)
    live_count = jnp.sum(is_live, axis=1).astype(jnp.int32)[:, None]
    edge_pos = jnp.broadcast_to(jnp.arange(edge_count, dtype=jnp.int32)[None, :], (N_SPACE, edge_count))
    picked = jax.random.randint(key_list[1], (N_SPACE, edge_count), 0, live_count)
    remote_any = MN + jnp.take_along_axis(live_order, picked, axis=1)
    own_any = jax.random.randint(key_list[2], (N_SPACE, edge_count), 0, MN)
    coin_flip = jax.random.randint(key_list[3], (N_SPACE, edge_count), 0, 2)
    chosen = jnp.where(coin_flip == 0, own_any, remote_any)
    covered = MN + jnp.take_along_axis(live_order, jnp.minimum(edge_pos, slot_count - 1), axis=1)
    chosen = jnp.where(edge_pos < live_count + MN, edge_pos - live_count, chosen)
    chosen = jnp.where(edge_pos < live_count, covered, chosen)
    scores = jax.random.randint(key_list[4], (N_SPACE, edge_count), 0, 1 << 16) * edge_count + edge_pos
    shuffle = jnp.argsort(scores, axis=1).astype(jnp.int32)
    chosen = jnp.take_along_axis(chosen, shuffle, axis=1)
    return jnp.transpose(chosen.reshape(N_SPACE, NEI, GP), (1, 0, 2)).reshape(NEI, GRID).astype(jnp.int32)


def draw_lat_row(key, part):
    key = jax.random.fold_in(key, 23)
    position = jnp.arange(GRID, dtype=jnp.int32)
    device_of = position // GP
    within = position % GP
    low_row = device_of * LATS // N_SPACE
    high_row = (device_of + 1) * LATS // N_SPACE
    band_width = jnp.maximum(high_row - low_row, 1)
    raw_bits = jax.random.randint(key, (GRID,), 0, 1 << 20)
    lat_rows = low_row + raw_bits % band_width
    lat_rows = jnp.where(within == 0, high_row - 1, lat_rows)
    lat_rows = jnp.where(within == 1, low_row, lat_rows)
    return lat_rows.astype(jnp.int32)


def with_ends(entries, own_key, low, top_value):
    dims = entries.shape
    index_at = [jax.random.randint(jax.random.fold_in(own_key, axis), (), 0, dims[axis]) for axis in range(len(dims))]
    entries = entries.at[tuple(index_at)].set(low)
    longest = dims.index(max(dims))
    index_at[longest] = (index_at[longest] + 1) % dims[longest]
    return entries.at[tuple(index_at)].set(top_value)


def block_levels(rng, shape, cuts, low, high):
    def one(dim, shards_of):
        draws = jax.random.uniform(jax.random.fold_in(jax.random.fold_in(rng, 6), dim), (shards_of,), jnp.float32, low / len(cuts), high / len(cuts))
        return jnp.repeat(jnp.exp(draws), shape[dim] // shards_of).reshape((-1,) + (1,) * (len(shape) - dim - 1))

    gain = one(*cuts[0])
    for cut in cuts[1:]:
        gain = gain * one(*cut)
    return gain


def noise(own_key, dims, spread, reach, cuts=(), kind=jnp.bfloat16):
    entries = jax.random.normal(own_key, dims, jnp.float32) * spread
    if len(cuts) > 0:
        entries = block_levels(own_key, dims, cuts, -0.22, 0.18) * entries
    return jnp.clip(entries, min=-reach, max=reach).astype(kind)


def setup_inputs(seed: int = 0, part: int = 0) -> dict:
    seeds = jax.random.split(jax.random.key(seed), 12)
    part_splits = jax.random.split(jax.random.fold_in(seeds[11], part), 12)
    grid_latent = noise(part_splits[0], (MEMBERS, GRID, LATENT), 1.0, 6.0, ((1, 16),))
    mesh_latent = noise(part_splits[1], (MEMBERS, MESH, LATENT), 1.0, 6.0, ((1, 16),))
    send_rows = with_ends(jax.random.randint(part_splits[2], (N_SPACE, N_SPACE, CAP), 0, MN), jax.random.fold_in(part_splits[2], 1), 0, MN - 1).astype(jnp.int32)
    edge_slot = draw_edge_slot(jax.random.fold_in(jax.random.fold_in(seeds[11], part), 71), part)
    lat_row = draw_lat_row(jax.random.fold_in(jax.random.fold_in(seeds[11], part), 71), part)
    verifying_analyses = noise(part_splits[5], (CHANNELS, GRID), 1.0, 6.0, ((1, 16),), jnp.float32)
    w_send = noise(seeds[6], (LATENT, HIDDEN_SIZE), (2 * LATENT) ** -0.5, 0.1875)
    w_recv = noise(seeds[7], (LATENT, HIDDEN_SIZE), (2 * LATENT) ** -0.5, 0.1875)
    w_edge = noise(seeds[8], (HIDDEN_SIZE, LATENT), HIDDEN_SIZE ** -0.5, 0.25)
    edge_gain = jnp.clip(1.0 + 0.18 * jax.random.normal(seeds[9], (LATENT,), jnp.float32), 0.1, 1.9)
    head_matrix = noise(seeds[10], (LATENT, CHANNELS), LATENT ** -0.5, 0.25)
    return dict(grid_latent=grid_latent, mesh_latent=mesh_latent, send_rows=send_rows, edge_slot=edge_slot, lat_row=lat_row, verifying_analyses=verifying_analyses, w_send=w_send, w_recv=w_recv, w_edge=w_edge, edge_gain=edge_gain, head_matrix=head_matrix)


DELTA_SQ = 0.0025
NORM_EPS = 1e-05
PRECISE = lax.Precision.HIGHEST

def head_matmul_result(form, left, right):
    return jnp.einsum(form, left.astype(jnp.float32), right.astype(jnp.float32), precision=PRECISE)

def softened_absolute(offset):
    return jnp.sqrt(offset * offset + DELTA_SQ)

def smooth_sign_function(offset):
    return offset / jnp.sqrt(offset * offset + DELTA_SQ)

def silu_slope(offset):
    logistic = jax.nn.sigmoid(offset)
    return logistic * (1.0 + offset * (1.0 - logistic))

def lat_weights(lat_row):
    return jnp.cos(jnp.pi * ((lat_row.astype(jnp.float32) + 0.5) / LATS - 0.5))

def table_ids(send_rows):
    device = jnp.arange(N_SPACE, dtype=jnp.int32)
    own_ids = device[:, None] * MN + jnp.arange(MN, dtype=jnp.int32)[None, :]
    remote_ids = device[:, None, None] * MN + send_rows.astype(jnp.int32)
    remote_ids = jnp.transpose(remote_ids, (1, 0, 2)).reshape(N_SPACE, N_SPACE * CAP)
    return jnp.concatenate([own_ids, remote_ids.astype(jnp.int32)], axis=1)

def local_pass(lookup, grid_rows, slot_ids, lat_weight, verifying_analyses, w_recv, w_edge, edge_gain, head_matrix, weight_sum, grid_total):
    member_outputs = grid_rows.shape[0]
    receiver = head_matmul_result('mgl,lh->mgh', grid_rows, w_recv)
    pre_acts = []
    hidden_acts = []
    normed_list = []
    inv_stds = []
    summed = jnp.zeros(grid_rows.shape, jnp.float32)
    for edge_index in range(slot_ids.shape[0]):
        pre_act = jnp.take(lookup, slot_ids[edge_index], axis=1).astype(jnp.float32) + receiver
        hidden_act = jax.nn.silu(pre_act).astype(jnp.bfloat16)
        edge_out = head_matmul_result('mgh,hl->mgl', hidden_act, w_edge)
        centred = edge_out - lax.optimization_barrier(jnp.mean(edge_out, axis=-1, keepdims=True))
        inv_std = lax.rsqrt(lax.optimization_barrier(jnp.mean(centred * centred, axis=-1, keepdims=True)) + NORM_EPS)
        normed = centred * inv_std
        summed = summed + normed * edge_gain
        pre_acts.append(pre_act)
        hidden_acts.append(hidden_act)
        normed_list.append(normed)
        inv_stds.append(inv_std)
    refreshed_latent = (grid_rows.astype(jnp.float32) + summed).astype(jnp.bfloat16)
    prognosis_values = head_matmul_result('ozw,wd->odz', refreshed_latent, head_matrix)
    accuracy_term = lax.optimization_barrier(jnp.mean(softened_absolute(prognosis_values - verifying_analyses[None]), axis=0))
    member_spread = lax.optimization_barrier(jnp.sum(softened_absolute(prognosis_values[:, None] - prognosis_values[None, :]), axis=(0, 1))) / (2.0 * member_outputs * (member_outputs - 1))
    crps_value = accuracy_term - member_spread
    weighted = jnp.sum(lat_weight * lax.optimization_barrier(jnp.sum(crps_value, axis=0)))
    dispersion_factor = lat_weight * (grid_total / weight_sum)
    couple_derivative = lax.optimization_barrier(jnp.sum(smooth_sign_function(prognosis_values[:, None] - prognosis_values[None, :]), axis=1)) / (member_outputs - 1)
    prognosis_sensitivity = (dispersion_factor * (smooth_sign_function(prognosis_values - verifying_analyses[None]) - couple_derivative)).astype(jnp.bfloat16)
    head_matrix_sensitivity = head_matmul_result('wuj,wru->jr', refreshed_latent, prognosis_sensitivity)
    refreshed_latent_adjoint = head_matmul_result('ord,ur->odu', prognosis_sensitivity, head_matrix)
    scaled_grad = refreshed_latent_adjoint * edge_gain
    grad_gain = jnp.zeros(edge_gain.shape, jnp.float32)
    grad_edge = jnp.zeros(w_edge.shape, jnp.float32)
    dreceiver = jnp.zeros(receiver.shape, jnp.float32)
    dpre_list = []
    for edge_index in range(slot_ids.shape[0]):
        normed = normed_list[edge_index]
        grad_gain = grad_gain + lax.optimization_barrier(jnp.sum(refreshed_latent_adjoint * normed, axis=(0, 1)))
        dedge = inv_stds[edge_index] * (scaled_grad - lax.optimization_barrier(jnp.mean(scaled_grad, axis=-1, keepdims=True)) - normed * lax.optimization_barrier(jnp.mean(scaled_grad * normed, axis=-1, keepdims=True)))
        dedge = dedge.astype(jnp.bfloat16)
        grad_edge = grad_edge + head_matmul_result('mgh,mgl->hl', hidden_acts[edge_index], dedge)
        dhidden = head_matmul_result('mgl,hl->mgh', dedge, w_edge)
        dpre = (dhidden * silu_slope(pre_acts[edge_index])).astype(jnp.bfloat16)
        dreceiver = dreceiver + dpre.astype(jnp.float32)
        dpre_list.append(dpre)
    dreceiver = dreceiver.astype(jnp.bfloat16)
    grad_grid = (refreshed_latent_adjoint + head_matmul_result('mgh,lh->mgl', dreceiver, w_recv)).astype(jnp.bfloat16)
    grad_recv = head_matmul_result('mgl,mgh->lh', grid_rows, dreceiver)
    flat_slots = slot_ids.reshape(-1)
    onehot = (flat_slots[None, :] == jnp.arange(lookup.shape[1], dtype=jnp.int32)[:, None]).astype(jnp.float32)
    dslot = head_matmul_result('ts,msh->mth', onehot, jnp.concatenate(dpre_list, axis=1)).astype(jnp.bfloat16)
    return (weighted, grad_grid, dslot, grad_recv, grad_edge, grad_gain, head_matrix_sensitivity)

def reference(grid_latent, mesh_latent, send_rows, edge_slot, lat_row, verifying_analyses, w_send, w_recv, w_edge, edge_gain, head_matrix):
    sender = head_matmul_result('mrl,lh->mrh', mesh_latent, w_send).astype(jnp.bfloat16)
    row_table = table_ids(send_rows)
    weight_all = lat_weights(lat_row)
    weight_sum = jnp.sum(weight_all)
    grid_blocks = jnp.transpose(grid_latent.reshape(MEMBERS, N_SPACE, GP, LATENT), (1, 0, 2, 3))
    slot_blocks = jnp.transpose(edge_slot.reshape(NEI, N_SPACE, GP), (1, 0, 2))
    weight_blocks = weight_all.reshape(N_SPACE, GP)
    target_blocks = jnp.transpose(verifying_analyses.reshape(CHANNELS, N_SPACE, GP), (1, 0, 2))

    def scan_step(carried, inputs):
        weighted, dsender, grad_recv, grad_edge, grad_gain, head_matrix_sensitivity = carried
        grid_rows, slot_ids, lat_weight, target_rows, row_ids = inputs
        lookup = jnp.take(sender, row_ids, axis=1)
        results = local_pass(lookup, grid_rows, slot_ids, lat_weight, target_rows, w_recv, w_edge, edge_gain, head_matrix, weight_sum, GRID)
        part_weighted, grad_grid, dslot, part_recv, part_edge, part_gain, part_out = results
        dsender = dsender.at[:, row_ids].add(dslot.astype(jnp.float32))
        carried = (weighted + part_weighted, dsender, grad_recv + part_recv, grad_edge + part_edge, grad_gain + part_gain, head_matrix_sensitivity + part_out)
        return (carried, grad_grid)
    initial = (jnp.zeros((), jnp.float32), jnp.zeros((MEMBERS, MESH, HIDDEN_SIZE), jnp.float32), jnp.zeros((LATENT, HIDDEN_SIZE), jnp.float32), jnp.zeros((HIDDEN_SIZE, LATENT), jnp.float32), jnp.zeros((LATENT,), jnp.float32), jnp.zeros((LATENT, CHANNELS), jnp.float32))
    carried, grid_grads = lax.scan(scan_step, initial, (grid_blocks, slot_blocks, weight_blocks, target_blocks, row_table))
    weighted, dsender, grad_recv, grad_edge, grad_gain, head_matrix_sensitivity = carried
    grad_grid = jnp.transpose(grid_grads, (1, 0, 2, 3)).reshape(MEMBERS, GRID, LATENT)
    grad_mesh = head_matmul_result('mrh,lh->mrl', dsender, w_send).astype(jnp.bfloat16)
    grad_send = head_matmul_result('mrl,mrh->lh', mesh_latent, dsender)
    loss = (weighted / weight_sum).reshape(1)
    return (loss, grad_grid, grad_mesh, grad_send, grad_recv, grad_edge, grad_gain, head_matrix_sensitivity)
```

```python
import functools

import jax
import jax.numpy as jnp
from jax import lax
from jax.experimental import pallas as pl
from jax.experimental.pallas import tpu as pltpu
from jax.sharding import PartitionSpec as P

LATS = 721


DELTA_SQ = 0.0025
NORM_EPS = 1e-05
PRECISE = lax.Precision.HIGHEST


def softened_absolute(offset):
    return jnp.sqrt(offset * offset + DELTA_SQ)


def smooth_sign_function(offset):
    return offset / jnp.sqrt(offset * offset + DELTA_SQ)


def silu_slope(offset):
    logistic = jax.nn.sigmoid(offset)
    return logistic * (1.0 + offset * (1.0 - logistic))


def project(node_rows, weight):
    return jnp.einsum("mrl,lh->mrh", node_rows, weight, preferred_element_type=jnp.float32).astype(
        jnp.bfloat16
    )


def fold_rows(returned, row_ids, row_count):
    onehot = (row_ids[None, :] == jnp.arange(row_count, dtype=jnp.int32)[:, None]).astype(
        returned.dtype
    )
    return jnp.einsum(
        "rs,msx->mrx", onehot, returned, preferred_element_type=jnp.float32, precision=PRECISE
    )


MESH_ID = pl.DeviceIdType.MESH
VMEM_LIMIT = 50 * 1024 * 1024


def greet_all(me, n):
    barrier = pltpu.get_barrier_semaphore()

    @pl.loop(1, n)
    def _(j):
        pl.semaphore_signal(
            barrier, inc=1, device_id={"space": lax.rem(me + j, n)}, device_id_type=MESH_ID
        )

    pl.semaphore_wait(barrier, n - 1)


def swap_blocks(me, n, source, target, send_sem, recv_sem, blockwise):
    @pl.loop(1, n)
    def _(j):
        peer = lax.rem(me + j, n)
        pltpu.make_async_remote_copy(
            src_ref=source.at[peer] if blockwise else source,
            dst_ref=target.at[me],
            send_sem=send_sem,
            recv_sem=recv_sem,
            device_id={"space": peer},
            device_id_type=MESH_ID,
        ).start()

    span = target.at[pl.ds(0, n - 1)]
    return pltpu.make_async_remote_copy(
        src_ref=span,
        dst_ref=span,
        send_sem=send_sem,
        recv_sem=recv_sem,
        device_id={"space": lax.rem(me + 1, n)},
        device_id_type=MESH_ID,
    )


def rows_kernel(n, sel_ref, mesh_ref, weight_ref, out_ref, weights_ref, outgoing, sems):
    me = lax.axis_index("space")
    greet_all(me, n)
    swap_weights = swap_blocks(me, n, weight_ref, weights_ref, sems.at[0], sems.at[1], False)
    weights_ref[me] = weight_ref[...]
    slots, width = outgoing.shape[1], outgoing.shape[2]
    sel = sel_ref[...]
    pick = (sel == lax.broadcasted_iota(jnp.int32, (sel.shape[0], mesh_ref.shape[0]), 1)).astype(
        jnp.bfloat16
    )
    rows = jnp.dot(pick, mesh_ref[...], preferred_element_type=jnp.float32).astype(jnp.bfloat16)
    outgoing[...] = rows.reshape(n, slots, width)
    swap_rows = swap_blocks(me, n, outgoing, out_ref, sems.at[2], sems.at[3], True)
    out_ref[me] = outgoing[me]
    swap_weights.wait()
    swap_rows.wait()


def exchange_rows(mesh_latent, send_rows, weight_part, n):
    members, own_rows, width = mesh_latent.shape
    cap = send_rows.shape[-1]
    rows = send_rows.reshape(n, 1, cap) + own_rows * jnp.arange(members, dtype=jnp.int32)[None, :, None]
    slots = members * cap
    return pl.pallas_call(
        functools.partial(rows_kernel, n),
        out_shape=(
            jax.ShapeDtypeStruct((n, slots, width), jnp.bfloat16),
            jax.ShapeDtypeStruct((n, 8, 128), jnp.float32),
        ),
        in_specs=[pl.BlockSpec(memory_space=pltpu.VMEM)] * 3,
        out_specs=[pl.BlockSpec(memory_space=pltpu.VMEM)] * 2,
        scratch_shapes=[
            pltpu.VMEM((n, slots, width), jnp.bfloat16),
            pltpu.SemaphoreType.DMA((4,)),
        ],
        compiler_params=pltpu.CompilerParams(
            collective_id=0, has_side_effects=True, vmem_limit_bytes=VMEM_LIMIT
        ),
    )(rows.reshape(n * slots, 1), mesh_latent.reshape(members * own_rows, width), weight_part)


def stream_bits(n):
    bits = [1 << k for k in range(n.bit_length() - 1)]
    return [bits, bits[:1] + bits[2:] + bits[1:2]]


def sum_kernel(
    n, x_ref, slot_ref, loss_ref, out_ref, ret_ref, losses_ref, work, landed, send_sems, recv_sems, sems
):
    me = lax.axis_index("space")
    greet_all(me, n)
    streams = stream_bits(n)
    steps = len(streams[0])
    total = x_ref.shape[1]
    low = [0] * len(streams)

    def remote(src, dst, s, k, bit):
        return pltpu.make_async_remote_copy(
            src_ref=src,
            dst_ref=dst,
            send_sem=send_sems.at[s, k],
            recv_sem=recv_sems.at[s, k],
            device_id={"space": jnp.bitwise_xor(me, bit)},
            device_id_type=MESH_ID,
        )

    def rows_at(start, size):
        return pl.ds(pl.multiple_of(start, 16), size)

    def halve(s, k):
        bit = streams[s][k]
        size = total >> (k + 1)
        mine = lax.rem(me // bit, 2)
        keep = low[s] + mine * size
        give = low[s] + (1 - mine) * size
        low[s] = keep
        source = x_ref if k == 0 else work
        copy = remote(
            source.at[s, rows_at(give, size)],
            landed.at[s, pl.ds(total - (total >> k), size)],
            s,
            k,
            bit,
        )
        copy.start()
        return copy

    def add(s, k):
        size = total >> (k + 1)
        source = x_ref if k == 0 else work
        target = out_ref if k == steps - 1 else work
        kept = rows_at(low[s], size)
        value = source[s, kept, :].astype(jnp.float32) + landed[
            s, pl.ds(total - (total >> k), size), :
        ].astype(jnp.float32)
        target[s, kept, :] = value.astype(jnp.bfloat16)

    def spread(s, k):
        bit = streams[s][k]
        size = total >> (k + 1)
        block = out_ref.at[s, rows_at(low[s], size)]
        copy = remote(block, block, s, 2 * steps - 1 - k, bit)
        copy.start()
        low[s] = low[s] - lax.rem(me // bit, 2) * size
        return copy

    copies = [halve(s, 0) for s in range(len(streams))]
    swap_slots = swap_blocks(me, n, slot_ref, ret_ref, sems.at[0], sems.at[1], True)
    swap_losses = swap_blocks(me, n, loss_ref, losses_ref, sems.at[2], sems.at[3], False)
    ret_ref[me] = slot_ref[me]
    losses_ref[me] = loss_ref[...]
    for k in range(steps):
        for s in range(len(streams)):
            copies[s].wait()
            add(s, k)
            copies[s] = halve(s, k + 1) if k < steps - 1 else spread(s, k)
    for k in reversed(range(steps)):
        for s in range(len(streams)):
            copies[s].wait()
            if k > 0:
                copies[s] = spread(s, k - 1)
    swap_slots.wait()
    swap_losses.wait()


def sum_over_space(x, slots, loss, n):
    streams = len(stream_bits(n))
    steps = n.bit_length() - 1
    return pl.pallas_call(
        functools.partial(sum_kernel, n),
        out_shape=(
            jax.ShapeDtypeStruct(x.shape, x.dtype),
            jax.ShapeDtypeStruct(slots.shape, slots.dtype),
            jax.ShapeDtypeStruct((n,) + loss.shape, loss.dtype),
        ),
        in_specs=[pl.BlockSpec(memory_space=pltpu.VMEM)] * 3,
        out_specs=[pl.BlockSpec(memory_space=pltpu.VMEM)] * 3,
        scratch_shapes=[
            pltpu.VMEM(x.shape, x.dtype),
            pltpu.VMEM(x.shape, x.dtype),
            pltpu.SemaphoreType.DMA((streams, 2 * steps)),
            pltpu.SemaphoreType.DMA((streams, 2 * steps)),
            pltpu.SemaphoreType.DMA((4,)),
        ],
        compiler_params=pltpu.CompilerParams(
            collective_id=1, has_side_effects=True, vmem_limit_bytes=VMEM_LIMIT
        ),
    )(x, slots, loss)


def corner(value):
    return jnp.broadcast_to(value.reshape(1, 1), (8, 128)).astype(jnp.float32)


def split_columns(parts, n):
    rows = sum(part.shape[0] for part in parts)
    total = -(-rows // (16 * n)) * 16 * n
    width = parts[0].shape[1]
    parts = parts + [jnp.zeros((total - rows, width), jnp.float32)]
    stacked = jnp.concatenate([part.astype(jnp.bfloat16) for part in parts], axis=0)
    half = width // 2
    return jnp.stack([stacked[:, :half], stacked[:, half:]])


def body(
    grid_latent,
    mesh_latent,
    send_rows,
    edge_slot,
    lat_row,
    verifying_analyses,
    w_send,
    w_recv,
    w_edge,
    edge_gain,
    head_matrix,
):
    member_outputs = grid_latent.shape[0]
    points = grid_latent.shape[1]
    own_rows = mesh_latent.shape[1]
    peer_count = lax.axis_size("space")
    outgoing = send_rows.reshape(-1)
    cap = send_rows.shape[-1]
    lat_weight = jnp.cos(jnp.pi * ((lat_row.astype(jnp.float32) + 0.5) / LATS - 0.5))
    arrived, weight_parts = exchange_rows(
        mesh_latent, send_rows, corner(jnp.sum(lat_weight)), peer_count
    )
    weight_sum = jnp.sum(weight_parts[:, 0, 0])
    arrived = jnp.transpose(
        arrived.reshape(peer_count, member_outputs, cap, -1), (1, 0, 2, 3)
    ).reshape(member_outputs, peer_count * cap, -1)
    gathered = jnp.concatenate([mesh_latent, arrived], axis=1)
    lookup = project(gathered, w_send)
    receiver = jnp.einsum("mgl,lh->mgh", grid_latent, w_recv, preferred_element_type=jnp.float32)
    pre_acts = []
    hidden_acts = []
    normed_list = []
    inv_stds = []
    summed = jnp.zeros(grid_latent.shape, jnp.float32)
    for edge_index in range(edge_slot.shape[0]):
        pre_act = jnp.take(lookup, edge_slot[edge_index], axis=1).astype(jnp.float32) + receiver
        hidden_act = jax.nn.silu(pre_act).astype(jnp.bfloat16)
        edge_out = jnp.einsum("mgh,hl->mgl", hidden_act, w_edge, preferred_element_type=jnp.float32)
        centred = edge_out - jnp.mean(edge_out, axis=-1, keepdims=True)
        inv_std = lax.rsqrt(jnp.mean(centred * centred, axis=-1, keepdims=True) + NORM_EPS)
        normed = centred * inv_std
        summed = summed + normed * edge_gain
        pre_acts.append(pre_act)
        hidden_acts.append(hidden_act)
        normed_list.append(normed)
        inv_stds.append(inv_std)
    refreshed_latent = (grid_latent.astype(jnp.float32) + summed).astype(jnp.bfloat16)
    prognosis_values = jnp.einsum(
        "ozw,wd->odz", refreshed_latent, head_matrix, preferred_element_type=jnp.float32
    )
    accuracy_term = jnp.mean(softened_absolute(prognosis_values - verifying_analyses[None]), axis=0)
    member_spread = jnp.sum(
        softened_absolute(prognosis_values[:, None] - prognosis_values[None, :]), axis=(0, 1)
    ) / (2.0 * member_outputs * (member_outputs - 1))
    crps_value = accuracy_term - member_spread
    weighted = jnp.sum(lat_weight * jnp.sum(crps_value, axis=0))
    dispersion_factor = lat_weight * (points * peer_count / weight_sum)
    couple_derivative = jnp.sum(
        smooth_sign_function(prognosis_values[:, None] - prognosis_values[None, :]), axis=1
    ) / (member_outputs - 1)
    prognosis_sensitivity = (
        dispersion_factor
        * (smooth_sign_function(prognosis_values - verifying_analyses[None]) - couple_derivative)
    ).astype(jnp.bfloat16)
    head_matrix_sensitivity = jnp.einsum(
        "wru,wuj->rj", prognosis_sensitivity, refreshed_latent, preferred_element_type=jnp.float32
    )
    refreshed_latent_adjoint = jnp.einsum(
        "ord,ur->odu", prognosis_sensitivity, head_matrix, preferred_element_type=jnp.float32
    )
    scaled_grad = refreshed_latent_adjoint * edge_gain
    grad_gain = jnp.zeros(edge_gain.shape, jnp.float32)
    grad_edge = jnp.zeros(w_edge.shape, jnp.float32)
    dreceiver = jnp.zeros(receiver.shape, jnp.float32)
    dpre_list = []
    for edge_index in range(edge_slot.shape[0]):
        normed = normed_list[edge_index]
        grad_gain = grad_gain + jnp.sum(refreshed_latent_adjoint * normed, axis=(0, 1))
        dedge = inv_stds[edge_index] * (
            scaled_grad
            - jnp.mean(scaled_grad, axis=-1, keepdims=True)
            - normed * jnp.mean(scaled_grad * normed, axis=-1, keepdims=True)
        )
        dedge = dedge.astype(jnp.bfloat16)
        grad_edge = grad_edge + jnp.einsum(
            "mgh,mgl->hl", hidden_acts[edge_index], dedge, preferred_element_type=jnp.float32
        )
        dhidden = jnp.einsum("mgl,hl->mgh", dedge, w_edge, preferred_element_type=jnp.float32)
        dpre = (dhidden * silu_slope(pre_acts[edge_index])).astype(jnp.bfloat16)
        dreceiver = dreceiver + dpre.astype(jnp.float32)
        dpre_list.append(dpre)
    dreceiver = dreceiver.astype(jnp.bfloat16)
    grad_grid = (
        refreshed_latent_adjoint
        + jnp.einsum("mgh,lh->mgl", dreceiver, w_recv, preferred_element_type=jnp.float32)
    ).astype(jnp.bfloat16)
    grad_recv = jnp.einsum(
        "mgl,mgh->lh", grid_latent, dreceiver, preferred_element_type=jnp.float32
    )
    flat_slots = edge_slot.reshape(-1)
    onehot = (flat_slots[None, :] == jnp.arange(lookup.shape[1], dtype=jnp.int32)[:, None]).astype(
        jnp.bfloat16
    )
    dslot = jnp.einsum(
        "ts,msh->mth",
        onehot,
        jnp.concatenate(dpre_list, axis=1),
        preferred_element_type=jnp.float32,
    ).astype(jnp.bfloat16)
    grad_send = jnp.einsum("mtl,mth->lh", gathered, dslot, preferred_element_type=jnp.float32)
    grad_lat = jnp.einsum("mth,lh->mtl", dslot, w_send, preferred_element_type=jnp.float32)
    slots = jnp.transpose(
        grad_lat[:, own_rows:].astype(jnp.bfloat16).reshape(member_outputs, peer_count, cap, -1),
        (1, 0, 2, 3),
    ).reshape(peer_count, member_outputs * cap, -1)
    parts = [grad_send, grad_recv, grad_edge, grad_gain[None], head_matrix_sensitivity]
    sums, returned, losses = sum_over_space(
        split_columns(parts, peer_count), slots, corner(weighted), peer_count
    )
    returned = jnp.transpose(
        returned.reshape(peer_count, member_outputs, cap, -1), (1, 0, 2, 3)
    ).reshape(member_outputs, peer_count * cap, -1)
    grad_mesh = grad_lat[:, :own_rows] + fold_rows(returned.astype(jnp.float32), outgoing, own_rows)
    sums = jnp.concatenate([sums[0], sums[1]], axis=1).astype(jnp.float32)
    totals = []
    start = 0
    for part in parts:
        totals.append(sums[start : start + part.shape[0]])
        start += part.shape[0]
    loss_value = (jnp.sum(losses[:, 0, 0]) / weight_sum).reshape(1)
    return (
        loss_value,
        grad_grid,
        grad_mesh.astype(jnp.bfloat16),
        totals[0],
        totals[1],
        totals[2],
        totals[3][0],
        totals[4].T,
    )


def solution(mesh):
    placed = (
        P(None, ("parts", "space"), None),
        P(None, ("parts", "space"), None),
        P(("parts", "space"), None, None),
        P(None, ("parts", "space")),
        P(("parts", "space")),
        P(None, ("parts", "space")),
        P(),
        P(),
        P(),
        P(),
        P(),
    )
    return jax.shard_map(
        body,
        mesh=mesh,
        in_specs=placed,
        out_specs=(
            P("parts"),
            P(None, ("parts", "space"), None),
            P(None, ("parts", "space"), None),
            P("parts", None),
            P("parts", None),
            P("parts", None),
            P("parts"),
            P("parts", None),
        ),
        check_vma=False,
    )
```

```python
import functools

import jax
import jax.numpy as jnp
from jax import lax
from jax.experimental import pallas as pl
from jax.experimental.pallas import tpu as pltpu
from jax.sharding import PartitionSpec as P

LATS = 721


DELTA_SQ = 0.0025
NORM_EPS = 1e-05
PRECISE = lax.Precision.HIGHEST


def fold_rows(returned, row_ids, row_count):
    onehot = (row_ids[None, :] == jnp.arange(row_count, dtype=jnp.int32)[:, None]).astype(
        returned.dtype
    )
    return jnp.einsum(
        "rs,msx->mrx", onehot, returned, preferred_element_type=jnp.float32, precision=PRECISE
    )


MESH_ID = pl.DeviceIdType.MESH
VMEM_LIMIT = 50 * 1024 * 1024


def greet_all(me, n):
    barrier = pltpu.get_barrier_semaphore()

    @pl.loop(1, n)
    def _(j):
        pl.semaphore_signal(
            barrier, inc=1, device_id={"space": lax.rem(me + j, n)}, device_id_type=MESH_ID
        )

    pl.semaphore_wait(barrier, n - 1)


def swap_blocks(me, n, source, target, send_sem, recv_sem, blockwise):
    @pl.loop(1, n)
    def _(j):
        peer = lax.rem(me + j, n)
        pltpu.make_async_remote_copy(
            src_ref=source.at[peer] if blockwise else source,
            dst_ref=target.at[me],
            send_sem=send_sem,
            recv_sem=recv_sem,
            device_id={"space": peer},
            device_id_type=MESH_ID,
        ).start()

    span = target.at[pl.ds(0, n - 1)]
    return pltpu.make_async_remote_copy(
        src_ref=span,
        dst_ref=span,
        send_sem=send_sem,
        recv_sem=recv_sem,
        device_id={"space": lax.rem(me + 1, n)},
        device_id_type=MESH_ID,
    )


def rows_kernel(n, sel_ref, mesh_ref, weight_ref, out_ref, weights_ref, outgoing, sems):
    me = lax.axis_index("space")
    greet_all(me, n)
    swap_weights = swap_blocks(me, n, weight_ref, weights_ref, sems.at[0], sems.at[1], False)
    weights_ref[me] = weight_ref[...]
    slots, width = outgoing.shape[1], outgoing.shape[2]
    sel = sel_ref[...]
    pick = (sel == lax.broadcasted_iota(jnp.int32, (sel.shape[0], mesh_ref.shape[0]), 1)).astype(
        jnp.bfloat16
    )
    rows = jnp.dot(pick, mesh_ref[...], preferred_element_type=jnp.float32).astype(jnp.bfloat16)
    outgoing[...] = rows.reshape(n, slots, width)
    swap_rows = swap_blocks(me, n, outgoing, out_ref, sems.at[2], sems.at[3], True)
    out_ref[me] = outgoing[me]
    swap_weights.wait()
    swap_rows.wait()


def exchange_rows(mesh_latent, send_rows, weight_part, n):
    members, own_rows, width = mesh_latent.shape
    cap = send_rows.shape[-1]
    rows = send_rows.reshape(n, 1, cap) + own_rows * jnp.arange(members, dtype=jnp.int32)[None, :, None]
    slots = members * cap
    return pl.pallas_call(
        functools.partial(rows_kernel, n),
        out_shape=(
            jax.ShapeDtypeStruct((n, slots, width), jnp.bfloat16),
            jax.ShapeDtypeStruct((n, 8, 128), jnp.float32),
        ),
        in_specs=[pl.BlockSpec(memory_space=pltpu.VMEM)] * 3,
        out_specs=[pl.BlockSpec(memory_space=pltpu.VMEM)] * 2,
        scratch_shapes=[
            pltpu.VMEM((n, slots, width), jnp.bfloat16),
            pltpu.SemaphoreType.DMA((4,)),
        ],
        compiler_params=pltpu.CompilerParams(
            collective_id=0, has_side_effects=True, vmem_limit_bytes=VMEM_LIMIT
        ),
    )(rows.reshape(n * slots, 1), mesh_latent.reshape(members * own_rows, width), weight_part)


def stream_bits(n):
    bits = [1 << k for k in range(n.bit_length() - 1)]
    return [bits, bits[:1] + bits[2:] + bits[1:2]]


def sum_kernel(
    n, x_ref, slot_ref, loss_ref, out_ref, ret_ref, losses_ref, work, landed, send_sems, recv_sems, sems
):
    me = lax.axis_index("space")
    greet_all(me, n)
    streams = stream_bits(n)
    steps = len(streams[0])
    total = x_ref.shape[1]
    low = [0] * len(streams)

    def remote(src, dst, s, k, bit):
        return pltpu.make_async_remote_copy(
            src_ref=src,
            dst_ref=dst,
            send_sem=send_sems.at[s, k],
            recv_sem=recv_sems.at[s, k],
            device_id={"space": jnp.bitwise_xor(me, bit)},
            device_id_type=MESH_ID,
        )

    def rows_at(start, size):
        return pl.ds(pl.multiple_of(start, 16), size)

    def halve(s, k):
        bit = streams[s][k]
        size = total >> (k + 1)
        mine = lax.rem(me // bit, 2)
        keep = low[s] + mine * size
        give = low[s] + (1 - mine) * size
        low[s] = keep
        source = x_ref if k == 0 else work
        copy = remote(
            source.at[s, rows_at(give, size)],
            landed.at[s, pl.ds(total - (total >> k), size)],
            s,
            k,
            bit,
        )
        copy.start()
        return copy

    def add(s, k):
        size = total >> (k + 1)
        source = x_ref if k == 0 else work
        target = out_ref if k == steps - 1 else work
        kept = rows_at(low[s], size)
        value = source[s, kept, :].astype(jnp.float32) + landed[
            s, pl.ds(total - (total >> k), size), :
        ].astype(jnp.float32)
        target[s, kept, :] = value.astype(jnp.bfloat16)

    def spread(s, k):
        bit = streams[s][k]
        size = total >> (k + 1)
        block = out_ref.at[s, rows_at(low[s], size)]
        copy = remote(block, block, s, 2 * steps - 1 - k, bit)
        copy.start()
        low[s] = low[s] - lax.rem(me // bit, 2) * size
        return copy

    copies = [halve(s, 0) for s in range(len(streams))]
    swap_slots = swap_blocks(me, n, slot_ref, ret_ref, sems.at[0], sems.at[1], True)
    swap_losses = swap_blocks(me, n, loss_ref, losses_ref, sems.at[2], sems.at[3], False)
    ret_ref[me] = slot_ref[me]
    losses_ref[me] = loss_ref[...]
    for k in range(steps):
        for s in range(len(streams)):
            copies[s].wait()
            add(s, k)
            copies[s] = halve(s, k + 1) if k < steps - 1 else spread(s, k)
    for k in reversed(range(steps)):
        for s in range(len(streams)):
            copies[s].wait()
            if k > 0:
                copies[s] = spread(s, k - 1)
    swap_slots.wait()
    swap_losses.wait()


def sum_over_space(x, slots, loss, n):
    streams = len(stream_bits(n))
    steps = n.bit_length() - 1
    return pl.pallas_call(
        functools.partial(sum_kernel, n),
        out_shape=(
            jax.ShapeDtypeStruct(x.shape, x.dtype),
            jax.ShapeDtypeStruct(slots.shape, slots.dtype),
            jax.ShapeDtypeStruct((n,) + loss.shape, loss.dtype),
        ),
        in_specs=[pl.BlockSpec(memory_space=pltpu.VMEM)] * 3,
        out_specs=[pl.BlockSpec(memory_space=pltpu.VMEM)] * 3,
        scratch_shapes=[
            pltpu.VMEM(x.shape, x.dtype),
            pltpu.VMEM(x.shape, x.dtype),
            pltpu.SemaphoreType.DMA((streams, 2 * steps)),
            pltpu.SemaphoreType.DMA((streams, 2 * steps)),
            pltpu.SemaphoreType.DMA((4,)),
        ],
        compiler_params=pltpu.CompilerParams(
            collective_id=1, has_side_effects=True, vmem_limit_bytes=VMEM_LIMIT
        ),
    )(x, slots, loss)


TN = (((0,), (0,)), ((), ()))
NT = (((1,), (1,)), ((), ()))


def mxu(left, right, dims=(((1,), (0,)), ((), ()))):
    return lax.dot_general(left, right, dims, preferred_element_type=jnp.float32)


def local_kernel(
    channels,
    grid_total,
    grid_ref,
    table_ref,
    slot_ref,
    lat_ref,
    weights_ref,
    target_ref,
    w_send_ref,
    w_recv_ref,
    w_edge_ref,
    gain_ref,
    head_ref,
    grad_grid_ref,
    own_ref,
    away_ref,
    sums_ref,
    loss_ref,
    sender,
    slope,
    normed,
    inv_std,
    hidden,
    updated,
    forecast,
    dforecast,
    dedge,
    dreceiver,
    dslot,
    pick,
    edge_total,
):
    members, points, width = grid_ref.shape
    slots = table_ref.shape[1]
    own_rows = own_ref.shape[1]
    edges = slot_ref.shape[0]
    gain = gain_ref[...]
    half = width // 2

    for e in range(edges):
        row = slot_ref[pl.ds(e, 1), :]
        pick[:, e * points : (e + 1) * points] = (
            lax.broadcasted_iota(jnp.int32, (slots, points), 0) == row
        ).astype(jnp.bfloat16)

    group = max(1, min(members, 512 // slots))
    while members % group:
        group -= 1

    @pl.loop(0, members // group)
    def _(t):
        rows = table_ref[pl.ds(t * group, group)].reshape(group * slots, width)
        sent = mxu(rows, w_send_ref[...]).astype(jnp.bfloat16)
        sender[pl.ds(t * group, group)] = sent.reshape(group, slots, width)

    @pl.loop(0, members)
    def _(m):
        latent = grid_ref[m]
        receiver = mxu(latent, w_recv_ref[...])
        v = mxu(pick[...], sender[m], TN) + jnp.concatenate([receiver] * edges, axis=0)
        s = 0.5 * jnp.tanh(0.5 * v) + 0.5
        act = v * s
        slope[m] = s + act * (1.0 - s)
        act = act.astype(jnp.bfloat16)
        hidden[m] = act
        out = mxu(act, w_edge_ref[...])
        centred = out - jnp.mean(out, axis=-1, keepdims=True)
        inv = lax.rsqrt(jnp.mean(centred * centred, axis=-1, keepdims=True) + NORM_EPS)
        scaled = centred * inv
        normed[m] = scaled
        inv_std[m] = inv
        summed = scaled[:points]
        for e in range(1, edges):
            summed = summed + scaled[e * points : (e + 1) * points]
        fresh = (latent.astype(jnp.float32) + summed * gain).astype(jnp.bfloat16)
        updated[m] = fresh
        forecast[m] = mxu(fresh, head_ref[...])

    weight_sum = jnp.sum(weights_ref[...], axis=0)[:1, :]
    factor_scale = grid_total / weight_sum
    chunk = 16
    lanes = forecast.shape[2]
    real = lax.broadcasted_iota(jnp.int32, (chunk, lanes), 1) < channels

    def score(t, total):
        rows = pl.ds(pl.multiple_of(t * chunk, chunk), chunk)
        weight = lat_ref[rows, :]
        target = target_ref[rows, :]
        values = [forecast[m, rows, :] for m in range(members)]
        accuracy = jnp.zeros((chunk, lanes), jnp.float32)
        spread = jnp.zeros((chunk, lanes), jnp.float32)
        signs = []
        for m in range(members):
            offset = values[m] - target
            square = offset * offset + DELTA_SQ
            root = lax.rsqrt(square)
            accuracy = accuracy + square * root
            signs.append(offset * root)
        couples = [jnp.zeros((chunk, lanes), jnp.float32) for _ in range(members)]
        for m in range(members):
            for k in range(m + 1, members):
                offset = values[m] - values[k]
                square = offset * offset + DELTA_SQ
                root = lax.rsqrt(square)
                spread = spread + square * root
                sign = offset * root
                couples[m] = couples[m] + sign
                couples[k] = couples[k] - sign
        spread = (2.0 * spread + members * DELTA_SQ**0.5) / (2.0 * members * (members - 1))
        crps = jnp.where(real, weight * (accuracy / members - spread), 0.0)
        factor = weight * factor_scale
        for m in range(members):
            dforecast[m, rows, :] = (factor * (signs[m] - couples[m] / (members - 1))).astype(
                jnp.bfloat16
            )
        return total + crps

    total = lax.fori_loop(0, points // chunk, score, jnp.zeros((chunk, lanes), jnp.float32))
    total = jnp.sum(jnp.sum(total, axis=1, keepdims=True), axis=0, keepdims=True)
    loss_ref[...] = jnp.broadcast_to(total, loss_ref.shape)

    def backward(m, gain_total):
        dupdated = mxu(dforecast[m], head_ref[...], NT)
        scaled_grad = dupdated * gain
        shifted = scaled_grad - jnp.mean(scaled_grad, axis=-1, keepdims=True)
        norm_sum = jnp.zeros((points, width), jnp.float32)
        for e in range(edges):
            rows = slice(e * points, (e + 1) * points)
            norm = normed[m, rows, :]
            norm_sum = norm_sum + norm
            slant = jnp.mean(scaled_grad * norm, axis=-1, keepdims=True)
            dedge[m, rows, :] = (inv_std[m, rows, :] * (shifted - norm * slant)).astype(jnp.bfloat16)
        gain_total = gain_total + jnp.sum(dupdated * norm_sum, axis=0, keepdims=True)
        dhidden = mxu(dedge[m], w_edge_ref[...], NT)
        dpre = (dhidden * slope[m]).astype(jnp.bfloat16)
        drecv = dpre[:points].astype(jnp.float32)
        for e in range(1, edges):
            drecv = drecv + dpre[e * points : (e + 1) * points].astype(jnp.float32)
        drecv = drecv.astype(jnp.bfloat16)
        dreceiver[m] = drecv
        grad_grid_ref[m] = (dupdated + mxu(drecv, w_recv_ref[...], NT)).astype(jnp.bfloat16)
        dslot[m] = mxu(pick[...], dpre).astype(jnp.bfloat16)
        return gain_total

    gain_total = lax.fori_loop(0, members, backward, jnp.zeros((1, width), jnp.float32))

    def put(start, value):
        value = value.astype(jnp.bfloat16)
        rows = slice(start, start + value.shape[0])
        sums_ref[0, rows, :] = value[:, :half]
        sums_ref[1, rows, :] = value[:, half:]

    def total_of(left, right, lead):
        edge_total[...] = jnp.zeros_like(edge_total)

        @pl.loop(0, members // lead)
        def _(t):
            block = pl.ds(t * lead, lead)
            rows = lead * left.shape[1]
            edge_total[...] += mxu(
                left[block].reshape(rows, width), right[block].reshape(rows, width), TN
            )

        return edge_total[...]

    put(0, total_of(table_ref, dslot, group))
    put(width, total_of(grid_ref, dreceiver, 2))
    put(2 * width, total_of(hidden, dedge, 1))
    put(
        3 * width,
        mxu(
            dforecast[...].reshape(members * points, lanes),
            updated[...].reshape(members * points, width),
            TN,
        ),
    )
    start = 3 * width + lanes
    tail = sums_ref.shape[1] - start
    first = lax.broadcasted_iota(jnp.int32, (tail, width), 0) == 0
    put(start, jnp.where(first, jnp.broadcast_to(gain_total, (tail, width)), 0.0))

    @pl.loop(0, members // group)
    def _(t):
        block = pl.ds(t * group, group)
        back = mxu(dslot[block].reshape(group * slots, width), w_send_ref[...], NT)
        back = back.reshape(group, slots, width)
        own_ref[block] = back[:, :own_rows]
        away_ref[block] = back[:, own_rows:].astype(jnp.bfloat16)


def local_pass(
    grid_latent, table, edge_slot, lat_weight, weight_parts, target, w_send, w_recv, w_edge, gain, head, own_rows, n
):
    members, points, width = grid_latent.shape
    slots = table.shape[1]
    edges = edge_slot.shape[0]
    channels = head.shape[1]
    lanes = -(-channels // 128) * 128
    rows = 3 * width + lanes + 16
    rows = -(-rows // (16 * n)) * 16 * n
    lane_pad = ((0, 0), (0, lanes - channels))
    stacked = edges * points
    f32, bf16 = jnp.float32, jnp.bfloat16
    return pl.pallas_call(
        functools.partial(local_kernel, channels, points * n),
        out_shape=(
            jax.ShapeDtypeStruct(grid_latent.shape, bf16),
            jax.ShapeDtypeStruct((members, own_rows, width), f32),
            jax.ShapeDtypeStruct((members, slots - own_rows, width), bf16),
            jax.ShapeDtypeStruct((2, rows, width // 2), bf16),
            jax.ShapeDtypeStruct((8, 128), f32),
        ),
        in_specs=[pl.BlockSpec(memory_space=pltpu.VMEM)] * 11,
        out_specs=[pl.BlockSpec(memory_space=pltpu.VMEM)] * 5,
        scratch_shapes=[
            pltpu.VMEM((members, slots, width), bf16),
            pltpu.VMEM((members, stacked, width), f32),
            pltpu.VMEM((members, stacked, width), f32),
            pltpu.VMEM((members, stacked, 1), f32),
            pltpu.VMEM((members, stacked, width), bf16),
            pltpu.VMEM((members, points, width), bf16),
            pltpu.VMEM((members, points, lanes), f32),
            pltpu.VMEM((members, points, lanes), bf16),
            pltpu.VMEM((members, stacked, width), bf16),
            pltpu.VMEM((members, points, width), bf16),
            pltpu.VMEM((members, slots, width), bf16),
            pltpu.VMEM((slots, stacked), bf16),
            pltpu.VMEM((width, width), f32),
        ],
        compiler_params=pltpu.CompilerParams(vmem_limit_bytes=VMEM_LIMIT),
    )(
        grid_latent,
        table,
        edge_slot,
        jnp.broadcast_to(lat_weight[:, None], (points, lanes)),
        weight_parts,
        jnp.pad(target.T, lane_pad),
        w_send,
        w_recv,
        w_edge,
        gain[None],
        jnp.pad(head, lane_pad),
    )


def corner(value):
    return jnp.broadcast_to(value.reshape(1, 1), (8, 128)).astype(jnp.float32)


def body(
    grid_latent,
    mesh_latent,
    send_rows,
    edge_slot,
    lat_row,
    verifying_analyses,
    w_send,
    w_recv,
    w_edge,
    edge_gain,
    head_matrix,
):
    member_outputs = grid_latent.shape[0]
    own_rows = mesh_latent.shape[1]
    peer_count = lax.axis_size("space")
    outgoing = send_rows.reshape(-1)
    cap = send_rows.shape[-1]
    lat_weight = jnp.cos(jnp.pi * ((lat_row.astype(jnp.float32) + 0.5) / LATS - 0.5))
    arrived, weight_parts = exchange_rows(
        mesh_latent, send_rows, corner(jnp.sum(lat_weight)), peer_count
    )
    weight_sum = jnp.sum(weight_parts[:, 0, 0])
    arrived = jnp.transpose(
        arrived.reshape(peer_count, member_outputs, cap, -1), (1, 0, 2, 3)
    ).reshape(member_outputs, peer_count * cap, -1)
    gathered = jnp.concatenate([mesh_latent, arrived], axis=1)
    grad_grid, own_grad, away_grad, sums, weighted = local_pass(
        grid_latent,
        gathered,
        edge_slot,
        lat_weight,
        weight_parts,
        verifying_analyses,
        w_send,
        w_recv,
        w_edge,
        edge_gain,
        head_matrix,
        own_rows,
        peer_count,
    )
    slots = jnp.transpose(
        away_grad.reshape(member_outputs, peer_count, cap, -1), (1, 0, 2, 3)
    ).reshape(peer_count, member_outputs * cap, -1)
    sums, returned, losses = sum_over_space(sums, slots, weighted, peer_count)
    returned = jnp.transpose(
        returned.reshape(peer_count, member_outputs, cap, -1), (1, 0, 2, 3)
    ).reshape(member_outputs, peer_count * cap, -1)
    grad_mesh = own_grad + fold_rows(returned.astype(jnp.float32), outgoing, own_rows)
    width = w_send.shape[0]
    channels = head_matrix.shape[1]
    after = 3 * width + -(-channels // 128) * 128

    def whole(start, count):
        return jnp.concatenate(
            [sums[0, start : start + count], sums[1, start : start + count]], axis=1
        ).astype(jnp.float32)

    loss_value = (jnp.sum(losses[:, 0, 0]) / weight_sum).reshape(1)
    return (
        loss_value,
        grad_grid,
        grad_mesh.astype(jnp.bfloat16),
        whole(0, width),
        whole(width, width),
        whole(2 * width, width),
        whole(after, 1)[0],
        whole(3 * width, channels).T,
    )


def solution(mesh):
    placed = (
        P(None, ("parts", "space"), None),
        P(None, ("parts", "space"), None),
        P(("parts", "space"), None, None),
        P(None, ("parts", "space")),
        P(("parts", "space")),
        P(None, ("parts", "space")),
        P(),
        P(),
        P(),
        P(),
        P(),
    )
    return jax.shard_map(
        body,
        mesh=mesh,
        in_specs=placed,
        out_specs=(
            P("parts"),
            P(None, ("parts", "space"), None),
            P(None, ("parts", "space"), None),
            P("parts", None),
            P("parts", None),
            P("parts", None),
            P("parts"),
            P("parts", None),
        ),
        check_vma=False,
    )
```

```python
import functools

import jax
import jax.numpy as jnp
from jax import lax
from jax.experimental import pallas as pl
from jax.experimental.pallas import tpu as pltpu
from jax.sharding import PartitionSpec as P

LATS = 721


DELTA_SQ = 0.0025
NORM_EPS = 1e-05


MESH_ID = pl.DeviceIdType.MESH
VMEM_LIMIT = 50 * 1024 * 1024


TN = (((0,), (0,)), ((), ()))
NT = (((1,), (1,)), ((), ()))


def mxu(left, right, dims=(((1,), (0,)), ((), ()))):
    return lax.dot_general(left, right, dims, preferred_element_type=jnp.float32)


def greet_all(me, n):
    barrier = pltpu.get_barrier_semaphore()

    @pl.loop(1, n)
    def _(j):
        pl.semaphore_signal(
            barrier, inc=1, device_id={"space": lax.rem(me + j, n)}, device_id_type=MESH_ID
        )

    pl.semaphore_wait(barrier, n - 1)


def swap_blocks(me, n, source, target, send_sem, recv_sem, blockwise):
    @pl.loop(1, n)
    def _(j):
        peer = lax.rem(me + j, n)
        pltpu.make_async_remote_copy(
            src_ref=source.at[peer] if blockwise else source,
            dst_ref=target.at[me],
            send_sem=send_sem,
            recv_sem=recv_sem,
            device_id={"space": peer},
            device_id_type=MESH_ID,
        ).start()

    span = target.at[pl.ds(0, n - 1)]
    return pltpu.make_async_remote_copy(
        src_ref=span,
        dst_ref=span,
        send_sem=send_sem,
        recv_sem=recv_sem,
        device_id={"space": lax.rem(me + 1, n)},
        device_id_type=MESH_ID,
    )


def rows_kernel(n, sel_ref, mesh_ref, weight_ref, out_ref, weights_ref, outgoing, sems):
    me = lax.axis_index("space")
    greet_all(me, n)
    swap_weights = swap_blocks(me, n, weight_ref, weights_ref, sems.at[0], sems.at[1], False)
    weights_ref[me] = weight_ref[...]
    slots, width = outgoing.shape[1], outgoing.shape[2]
    sel = sel_ref[...]
    pick = (sel == lax.broadcasted_iota(jnp.int32, (sel.shape[0], mesh_ref.shape[0]), 1)).astype(
        jnp.bfloat16
    )
    rows = jnp.dot(pick, mesh_ref[...], preferred_element_type=jnp.float32).astype(jnp.bfloat16)
    outgoing[...] = rows.reshape(n, slots, width)
    swap_rows = swap_blocks(me, n, outgoing, out_ref, sems.at[2], sems.at[3], True)
    out_ref[me] = outgoing[me]
    swap_weights.wait()
    swap_rows.wait()


def sent_rows(send_rows, members, own_rows, n):
    cap = send_rows.shape[-1]
    rows = send_rows.reshape(n, 1, cap) + own_rows * jnp.arange(members, dtype=jnp.int32)[None, :, None]
    return rows.reshape(n * members * cap, 1)


def exchange_rows(mesh_latent, rows, weight_part, n):
    members, own_rows, width = mesh_latent.shape
    slots = rows.shape[0] // n
    return pl.pallas_call(
        functools.partial(rows_kernel, n),
        out_shape=(
            jax.ShapeDtypeStruct((n, slots, width), jnp.bfloat16),
            jax.ShapeDtypeStruct((n, 8, 128), jnp.float32),
        ),
        in_specs=[pl.BlockSpec(memory_space=pltpu.VMEM)] * 3,
        out_specs=[pl.BlockSpec(memory_space=pltpu.VMEM)] * 2,
        scratch_shapes=[
            pltpu.VMEM((n, slots, width), jnp.bfloat16),
            pltpu.SemaphoreType.DMA((4,)),
        ],
        compiler_params=pltpu.CompilerParams(
            collective_id=0, has_side_effects=True, vmem_limit_bytes=VMEM_LIMIT
        ),
    )(rows, mesh_latent.reshape(members * own_rows, width), weight_part)


STREAMS = 4
TOGETHER = 2


def stream_bits(n):
    bits = [1 << k for k in range(n.bit_length() - 1)]
    return [bits, bits[:1] + bits[2:] + bits[1:2]] * (STREAMS // 2)


def sum_kernel(
    n,
    x_ref,
    slot_ref,
    loss_ref,
    sel_ref,
    own_ref,
    out_ref,
    mesh_ref,
    losses_ref,
    work,
    landed,
    ret_ref,
    send_sems,
    recv_sems,
    sems,
):
    me = lax.axis_index("space")
    greet_all(me, n)
    streams = stream_bits(n)
    steps = len(streams[0])
    total = x_ref.shape[1]
    low = [0] * len(streams)

    def remote(src, dst, s, k, bit):
        return pltpu.make_async_remote_copy(
            src_ref=src,
            dst_ref=dst,
            send_sem=send_sems.at[s, k],
            recv_sem=recv_sems.at[s, k],
            device_id={"space": jnp.bitwise_xor(me, bit)},
            device_id_type=MESH_ID,
        )

    def rows_at(start, size):
        return pl.ds(pl.multiple_of(start, 16), size)

    def halve(s, k):
        bit = streams[s][k]
        size = total >> (k + 1)
        mine = lax.rem(me // bit, 2)
        keep = low[s] + mine * size
        give = low[s] + (1 - mine) * size
        low[s] = keep
        source = x_ref if k == 0 else work
        copy = remote(
            source.at[s, rows_at(give, size)],
            landed.at[s, pl.ds(total - (total >> k), size)],
            s,
            k,
            bit,
        )
        copy.start()
        return copy

    def add(s, k):
        size = total >> (k + 1)
        source = x_ref if k == 0 else work
        target = out_ref if k == steps - 1 else work
        kept = rows_at(low[s], size)
        value = source[s, kept, :].astype(jnp.float32) + landed[
            s, pl.ds(total - (total >> k), size), :
        ].astype(jnp.float32)
        target[s, kept, :] = value.astype(jnp.bfloat16)

    def spread(s, k):
        bit = streams[s][k]
        size = total >> (k + 1)
        block = out_ref.at[s, rows_at(low[s], size)]
        copy = remote(block, block, s, 2 * steps - 1 - k, bit)
        copy.start()
        low[s] = low[s] - lax.rem(me // bit, 2) * size
        return copy

    copies = [halve(s, 0) for s in range(len(streams))]
    swap_slots = swap_blocks(me, n, slot_ref, ret_ref, sems.at[0], sems.at[1], True)
    swap_losses = swap_blocks(me, n, loss_ref, losses_ref, sems.at[2], sems.at[3], False)
    ret_ref[me] = slot_ref[me]
    losses_ref[me] = loss_ref[...]
    for k in range(2 * steps):
        for s in range(len(streams)):
            copies[s].wait()
            if k < steps:
                add(s, k)
            if k < steps - 1:
                copies[s] = halve(s, k + 1)
            elif k < 2 * steps - 1:
                copies[s] = spread(s, 2 * steps - 2 - k)
        if k == steps - 1:
            swap_slots.wait()
            members, own_rows, width = own_ref.shape
            sel = sel_ref[...]
            pick = (
                sel == lax.broadcasted_iota(jnp.int32, (sel.shape[0], members * own_rows), 1)
            ).astype(jnp.bfloat16)
            back = mxu(pick, ret_ref[...].reshape(sel.shape[0], width), TN)
            mesh_ref[...] = (own_ref[...] + back.reshape(own_ref.shape)).astype(jnp.bfloat16)
    swap_losses.wait()


def sum_over_space(x, slots, loss, rows, own, n):
    steps = n.bit_length() - 1
    return pl.pallas_call(
        functools.partial(sum_kernel, n),
        out_shape=(
            jax.ShapeDtypeStruct(x.shape, x.dtype),
            jax.ShapeDtypeStruct(own.shape, slots.dtype),
            jax.ShapeDtypeStruct((n,) + loss.shape, loss.dtype),
        ),
        in_specs=[pl.BlockSpec(memory_space=pltpu.VMEM)] * 5,
        out_specs=[pl.BlockSpec(memory_space=pltpu.VMEM)] * 3,
        scratch_shapes=[
            pltpu.VMEM(x.shape, x.dtype),
            pltpu.VMEM(x.shape, x.dtype),
            pltpu.VMEM(slots.shape, slots.dtype),
            pltpu.SemaphoreType.DMA((STREAMS, 2 * steps)),
            pltpu.SemaphoreType.DMA((STREAMS, 2 * steps)),
            pltpu.SemaphoreType.DMA((4,)),
        ],
        compiler_params=pltpu.CompilerParams(
            collective_id=1, has_side_effects=True, vmem_limit_bytes=VMEM_LIMIT
        ),
    )(x, slots, loss, rows, own)


def local_kernel(
    channels,
    grid_total,
    grid_ref,
    table_ref,
    slot_ref,
    lat_ref,
    weights_ref,
    target_ref,
    w_send_ref,
    w_recv_ref,
    w_edge_ref,
    gain_ref,
    head_ref,
    grad_grid_ref,
    own_ref,
    away_ref,
    sums_ref,
    loss_ref,
    sender,
    slope,
    normed,
    inv_std,
    hidden,
    updated,
    forecast,
    dforecast,
    dedge,
    dreceiver,
    dslot,
    pick,
    edge_total,
    truth,
):
    members, points, width = grid_ref.shape
    slots = table_ref.shape[1]
    own_rows = own_ref.shape[1]
    edges = slot_ref.shape[0]
    gain = gain_ref[...]
    part = sums_ref.shape[2]

    for e in range(edges):
        row = slot_ref[pl.ds(e, 1), :]
        pick[:, e * points : (e + 1) * points] = (
            lax.broadcasted_iota(jnp.int32, (slots, points), 0) == row
        ).astype(jnp.bfloat16)

    group = max(1, min(members, 512 // slots))
    while members % group:
        group -= 1

    @pl.loop(0, members // group)
    def _(t):
        rows = table_ref[pl.ds(t * group, group)].reshape(group * slots, width)
        sent = mxu(rows, w_send_ref[...]).astype(jnp.bfloat16)
        sender[pl.ds(t * group, group)] = sent.reshape(group, slots, width)

    def forward(m):
        latent = grid_ref[m]
        receiver = mxu(latent, w_recv_ref[...])
        v = mxu(pick[...], sender[m], TN) + jnp.concatenate([receiver] * edges, axis=0)
        s = 0.5 * jnp.tanh(0.5 * v) + 0.5
        act = v * s
        slope[m] = s + act * (1.0 - s)
        act = act.astype(jnp.bfloat16)
        hidden[m] = act
        out = mxu(act, w_edge_ref[...])
        centred = out - jnp.mean(out, axis=-1, keepdims=True)
        inv = lax.rsqrt(jnp.mean(centred * centred, axis=-1, keepdims=True) + NORM_EPS)
        scaled = centred * inv
        normed[m] = scaled
        inv_std[m] = inv
        summed = scaled[:points]
        for e in range(1, edges):
            summed = summed + scaled[e * points : (e + 1) * points]
        fresh = (latent.astype(jnp.float32) + summed * gain).astype(jnp.bfloat16)
        updated[m] = fresh
        forecast[m] = mxu(fresh, head_ref[...], NT)

    @pl.loop(0, members // TOGETHER)
    def _(t):
        for u in range(TOGETHER):
            forward(t * TOGETHER + u)

    truth[...] = target_ref[...].T
    weight_sum = jnp.sum(weights_ref[...], axis=0)[:1, :]
    factor_scale = grid_total / weight_sum
    chunk = 16
    lanes = forecast.shape[2]
    real = lax.broadcasted_iota(jnp.int32, (chunk, lanes), 1) < channels

    def score(t, total):
        rows = pl.ds(pl.multiple_of(t * chunk, chunk), chunk)
        weight = lat_ref[rows, :]
        target = truth[rows, :]
        values = [forecast[m, rows, :] for m in range(members)]
        accuracy = jnp.zeros((chunk, lanes), jnp.float32)
        spread = jnp.zeros((chunk, lanes), jnp.float32)
        signs = []
        for m in range(members):
            offset = values[m] - target
            square = offset * offset + DELTA_SQ
            root = lax.rsqrt(square)
            accuracy = accuracy + square * root
            signs.append(offset * root)
        couples = [jnp.zeros((chunk, lanes), jnp.float32) for _ in range(members)]
        for m in range(members):
            for k in range(m + 1, members):
                offset = values[m] - values[k]
                square = offset * offset + DELTA_SQ
                root = lax.rsqrt(square)
                spread = spread + square * root
                sign = offset * root
                couples[m] = couples[m] + sign
                couples[k] = couples[k] - sign
        spread = (2.0 * spread + members * DELTA_SQ**0.5) / (2.0 * members * (members - 1))
        crps = jnp.where(real, weight * (accuracy / members - spread), 0.0)
        factor = weight * factor_scale
        for m in range(members):
            dforecast[m, rows, :] = (factor * (signs[m] - couples[m] / (members - 1))).astype(
                jnp.bfloat16
            )
        return total + crps

    total = lax.fori_loop(0, points // chunk, score, jnp.zeros((chunk, lanes), jnp.float32))
    total = jnp.sum(jnp.sum(total, axis=1, keepdims=True), axis=0, keepdims=True)
    loss_ref[...] = jnp.broadcast_to(total, loss_ref.shape)

    def backward(m, gain_total):
        dupdated = mxu(dforecast[m], head_ref[...])
        scaled_grad = dupdated * gain
        shifted = scaled_grad - jnp.mean(scaled_grad, axis=-1, keepdims=True)
        norm_sum = jnp.zeros((points, width), jnp.float32)
        for e in range(edges):
            rows = slice(e * points, (e + 1) * points)
            norm = normed[m, rows, :]
            norm_sum = norm_sum + norm
            slant = jnp.mean(scaled_grad * norm, axis=-1, keepdims=True)
            dedge[m, rows, :] = (inv_std[m, rows, :] * (shifted - norm * slant)).astype(jnp.bfloat16)
        gain_total = gain_total + jnp.sum(dupdated * norm_sum, axis=0, keepdims=True)
        dhidden = mxu(dedge[m], w_edge_ref[...], NT)
        dpre = (dhidden * slope[m]).astype(jnp.bfloat16)
        drecv = dpre[:points].astype(jnp.float32)
        for e in range(1, edges):
            drecv = drecv + dpre[e * points : (e + 1) * points].astype(jnp.float32)
        drecv = drecv.astype(jnp.bfloat16)
        dreceiver[m] = drecv
        grad_grid_ref[m] = (dupdated + mxu(drecv, w_recv_ref[...], NT)).astype(jnp.bfloat16)
        dslot[m] = mxu(pick[...], dpre).astype(jnp.bfloat16)
        return gain_total

    def backward_group(t, gain_total):
        for u in range(TOGETHER):
            gain_total = backward(t * TOGETHER + u, gain_total)
        return gain_total

    gain_total = lax.fori_loop(
        0, members // TOGETHER, backward_group, jnp.zeros((1, width), jnp.float32)
    )

    def put(start, value):
        value = value.astype(jnp.bfloat16)
        rows = slice(start, start + value.shape[0])
        for s in range(sums_ref.shape[0]):
            sums_ref[s, rows, :] = value[:, s * part : (s + 1) * part]

    def total_of(left, right, lead):
        edge_total[...] = jnp.zeros_like(edge_total)

        @pl.loop(0, members // lead)
        def _(t):
            block = pl.ds(t * lead, lead)
            rows = lead * left.shape[1]
            edge_total[...] += mxu(
                left[block].reshape(rows, width), right[block].reshape(rows, width), TN
            )

        return edge_total[...]

    put(0, total_of(table_ref, dslot, group))
    put(width, total_of(grid_ref, dreceiver, 2))
    put(2 * width, total_of(hidden, dedge, 1))
    put(
        3 * width,
        mxu(
            dforecast[...].reshape(members * points, lanes),
            updated[...].reshape(members * points, width),
            TN,
        ),
    )
    start = 3 * width + lanes
    tail = sums_ref.shape[1] - start
    first = lax.broadcasted_iota(jnp.int32, (tail, width), 0) == 0
    put(start, jnp.where(first, jnp.broadcast_to(gain_total, (tail, width)), 0.0))

    @pl.loop(0, members // group)
    def _(t):
        block = pl.ds(t * group, group)
        back = mxu(dslot[block].reshape(group * slots, width), w_send_ref[...], NT)
        back = back.reshape(group, slots, width)
        own_ref[block] = back[:, :own_rows]
        away_ref[block] = back[:, own_rows:].astype(jnp.bfloat16)


def local_pass(
    grid_latent, table, edge_slot, lat_weight, weight_parts, target, w_send, w_recv, w_edge, gain, head, own_rows, n
):
    members, points, width = grid_latent.shape
    slots = table.shape[1]
    edges = edge_slot.shape[0]
    channels = head.shape[1]
    lanes = -(-channels // 128) * 128
    rows = 3 * width + lanes + 16
    rows = -(-rows // (16 * n)) * 16 * n
    stacked = edges * points
    f32, bf16 = jnp.float32, jnp.bfloat16
    return pl.pallas_call(
        functools.partial(local_kernel, channels, points * n),
        out_shape=(
            jax.ShapeDtypeStruct(grid_latent.shape, bf16),
            jax.ShapeDtypeStruct((members, own_rows, width), f32),
            jax.ShapeDtypeStruct((members, slots - own_rows, width), bf16),
            jax.ShapeDtypeStruct((STREAMS, rows, width // STREAMS), bf16),
            jax.ShapeDtypeStruct((8, 128), f32),
        ),
        in_specs=[pl.BlockSpec(memory_space=pltpu.VMEM)] * 11,
        out_specs=[pl.BlockSpec(memory_space=pltpu.VMEM)] * 5,
        scratch_shapes=[
            pltpu.VMEM((members, slots, width), bf16),
            pltpu.VMEM((members, stacked, width), f32),
            pltpu.VMEM((members, stacked, width), f32),
            pltpu.VMEM((members, stacked, 1), f32),
            pltpu.VMEM((members, stacked, width), bf16),
            pltpu.VMEM((members, points, width), bf16),
            pltpu.VMEM((members, points, lanes), f32),
            pltpu.VMEM((members, points, lanes), bf16),
            pltpu.VMEM((members, stacked, width), bf16),
            pltpu.VMEM((members, points, width), bf16),
            pltpu.VMEM((members, slots, width), bf16),
            pltpu.VMEM((slots, stacked), bf16),
            pltpu.VMEM((width, width), f32),
            pltpu.VMEM((points, lanes), f32),
        ],
        compiler_params=pltpu.CompilerParams(vmem_limit_bytes=VMEM_LIMIT),
    )(
        grid_latent,
        table,
        edge_slot,
        jnp.broadcast_to(lat_weight[:, None], (points, lanes)),
        weight_parts,
        jnp.pad(target, ((0, lanes - channels), (0, 0))),
        w_send,
        w_recv,
        w_edge,
        gain[None],
        jnp.pad(head.T, ((0, lanes - channels), (0, 0))),
    )


def corner(value):
    return jnp.broadcast_to(value.reshape(1, 1), (8, 128)).astype(jnp.float32)


def body(
    grid_latent,
    mesh_latent,
    send_rows,
    edge_slot,
    lat_row,
    verifying_analyses,
    w_send,
    w_recv,
    w_edge,
    edge_gain,
    head_matrix,
):
    member_outputs = grid_latent.shape[0]
    own_rows = mesh_latent.shape[1]
    peer_count = lax.axis_size("space")
    rows = sent_rows(send_rows, member_outputs, own_rows, peer_count)
    cap = send_rows.shape[-1]
    lat_weight = jnp.cos(jnp.pi * ((lat_row.astype(jnp.float32) + 0.5) / LATS - 0.5))
    arrived, weight_parts = exchange_rows(
        mesh_latent, rows, corner(jnp.sum(lat_weight)), peer_count
    )
    weight_sum = jnp.sum(weight_parts[:, 0, 0])
    arrived = jnp.transpose(
        arrived.reshape(peer_count, member_outputs, cap, -1), (1, 0, 2, 3)
    ).reshape(member_outputs, peer_count * cap, -1)
    gathered = jnp.concatenate([mesh_latent, arrived], axis=1)
    grad_grid, own_grad, away_grad, sums, weighted = local_pass(
        grid_latent,
        gathered,
        edge_slot,
        lat_weight,
        weight_parts,
        verifying_analyses,
        w_send,
        w_recv,
        w_edge,
        edge_gain,
        head_matrix,
        own_rows,
        peer_count,
    )
    slots = jnp.transpose(
        away_grad.reshape(member_outputs, peer_count, cap, -1), (1, 0, 2, 3)
    ).reshape(peer_count, member_outputs * cap, -1)
    sums, grad_mesh, losses = sum_over_space(sums, slots, weighted, rows, own_grad, peer_count)
    width = w_send.shape[0]
    channels = head_matrix.shape[1]
    after = 3 * width + -(-channels // 128) * 128

    def whole(start, count):
        return jnp.concatenate(
            [sums[s, start : start + count] for s in range(STREAMS)], axis=1
        ).astype(jnp.float32)

    loss_value = (jnp.sum(losses[:, 0, 0]) / weight_sum).reshape(1)
    return (
        loss_value,
        grad_grid,
        grad_mesh,
        whole(0, width),
        whole(width, width),
        whole(2 * width, width),
        whole(after, 1)[0],
        whole(3 * width, channels).T,
    )


def solution(mesh):
    placed = (
        P(None, ("parts", "space"), None),
        P(None, ("parts", "space"), None),
        P(("parts", "space"), None, None),
        P(None, ("parts", "space")),
        P(("parts", "space")),
        P(None, ("parts", "space")),
        P(),
        P(),
        P(),
        P(),
        P(),
    )
    return jax.shard_map(
        body,
        mesh=mesh,
        in_specs=placed,
        out_specs=(
            P("parts"),
            P(None, ("parts", "space"), None),
            P(None, ("parts", "space"), None),
            P("parts", None),
            P("parts", None),
            P("parts", None),
            P("parts"),
            P("parts", None),
        ),
        check_vma=False,
    )
```
